32 devices in a mesh: dp: 2 (over x), expert: 16 (over z, y, core).
Axes of the slice: x: 2, y: 2, z: 4, core: 2. Of those that a mesh axis runs over, the one named last changes fastest.
Arguments:
- tokens: bfloat16 [2048, 7168], P('expert', 'dp'), may hold values from -6 to 6
- cotangent: bfloat16 [2048, 7168], P('expert', 'dp'), may hold values from -6 to 6
- routes: int32 [2048, 4], P('expert'), may hold values from 0 to 15, all different within a row; in each aligned block of 128 rows (0 to 127, 128 to 255, ...) at most 48 rows name the same one
- combine_weights: float32 [2048, 4], P('expert'), may hold values from 0.2 to 1
- gate_weight: bfloat16 [16, 7168, 1024], P('expert', 'dp'), may hold values from -0.0625 to 0.0625
- up_weight: bfloat16 [16, 7168, 1024], P('expert', 'dp'), may hold values from -0.0625 to 0.0625
- down_weight: bfloat16 [16, 1024, 7168], P('expert', None, 'dp'), may hold values from -0.1875 to 0.1875
Outputs:
- grad_tokens: bfloat16 [2048, 7168], P('expert', 'dp')
- grad_gate: bfloat16 [16, 7168, 1024], P('expert', 'dp')
- grad_up: bfloat16 [16, 7168, 1024], P('expert', 'dp')
- grad_down: bfloat16 [16, 1024, 7168], P('expert', None, 'dp')
The draws below stay inside these ranges and needn't reach their ends.
Inputs may be any that keep to these rules, and one draw needn't show every extreme that they name: `routes`: each row names 4 different experts. Within each aligned block of 128 tokens no expert is named by more than 48 tokens, and in every draw some block has an expert named by exactly 48 tokens.
All inputs are finite; a program needn't handle non-finite values.
Results may differ from the reference program's by a relative error of at most 0.029.
Values may be sent and summed in bfloat16 or wider, within the bound.
A program may use at most 128 MiB of HBM per device.

```python
import math
import jax
import jax.numpy as jnp
import numpy as np
from jax import lax

D = 7168
HID = 1024
TOP = 4
TOK_DEV = 128
EXPERTS = 16
CAP = 48
TOKENS = 2048
N_DP = 2
N_EXPERT = 16


def shard_levels(rng, dims, split, low, high):
    factor_of = 1.0
    for position, shards_of in split:
        draws = jax.random.uniform(jax.random.fold_in(jax.random.fold_in(rng, 6), position), (shards_of,), jnp.float32, low / len(split), high / len(split))
        factor_of = factor_of * jnp.repeat(jnp.exp(draws), dims[position] // shards_of).reshape((-1,) + (1,) * (len(dims) - 1 - position))
    return factor_of


def assign_block(rng, own, number, rows, amount, top, most, skew):
    ranking = jax.random.permutation(rng, amount)
    crowded, usual = portions_of(amount, rows * top, most, skew, True), portions_of(amount, rows * top, most, skew, False)
    places = jnp.arange(amount)

    def named(tallies, offset_by):
        used = int((tallies > 0).sum())
        fixed = max(1, used // 4)
        moved = fixed + (places - fixed + offset_by * (used - fixed)) % max(1, amount - fixed)
        return jnp.zeros((amount,), jnp.int32).at[ranking[jnp.where(places < fixed, places, moved)]].set(jnp.asarray(tallies, jnp.int32))

    tallies = jnp.where(number % 4 == 0, named(crowded, number // 4), named(usual, number - number // 4 - 1))
    mixed = jax.random.permutation(jax.random.fold_in(own, 3), amount)
    donor, sink = mixed[0:amount // 2 * 2:2], mixed[1:amount // 2 * 2:2]
    slack = jnp.minimum(tallies[donor] - 1, most - tallies[sink]) // 2
    slack = jnp.where((donor == ranking[0]) | (sink == ranking[0]) | (tallies[sink] == 0), 0, jnp.maximum(slack, 0))
    moved = jax.random.randint(jax.random.fold_in(own, 4), (amount // 2,), 0, 1 << 20) % (slack + 1)
    tallies = tallies.at[donor].add(-moved).at[sink].add(moved)
    labels = jnp.searchsorted(jnp.cumsum(tallies), jnp.arange(rows * top), side="right").astype(jnp.int32)
    grid = labels.reshape(top, rows).T
    grid = grid[jax.random.permutation(jax.random.fold_in(own, 1), rows)]
    offset_by = jax.random.randint(jax.random.fold_in(own, 2), (rows, 1), 0, top)
    return jnp.take_along_axis(grid, (jnp.arange(top)[None, :] + offset_by) % top, axis=1)


def portions_of(amount, total, reach, lean, full):
    loads = [(1 << 20) // math.isqrt(rank ** lean) + 1 for rank in range(1, amount + 1)]
    largest = reach if full else min(reach, max(-(-total // amount), total * loads[0] // sum(loads)))
    least = 1 if total - largest >= amount - 1 else 0
    holding, spare = [largest] + [least] * (amount - 1), total - largest - least * (amount - 1)
    while spare > 0:
        movable = [i for i in range(1, amount) if holding[i] < largest] or [i for i in range(1, amount) if holding[i] < reach]
        mass, left = sum([loads[i] for i in movable]), spare
        for i in movable:
            extra = min(reach - holding[i], max(1, left * loads[i] // mass), spare)
            holding[i] = holding[i] + extra
            spare = spare - extra
    return np.array(holding)


def scatter_about(own_key, shape, spread, bound, pieces=(), kind=jnp.bfloat16):
    gain = shard_levels(own_key, shape, pieces, -0.22, 0.18) if pieces else 1.0
    entries = jax.random.normal(own_key, shape, jnp.float32) * spread * gain
    return jnp.minimum(jnp.maximum(entries, -bound), bound).astype(kind)


def setup_inputs(seed: int = 0) -> dict:
    arg_keys = jax.random.split(jax.random.key(seed), 8)
    tokens = scatter_about(arg_keys[0], (TOKENS, D), 1.0, 6.0, ((0, 16), (1, 2)))
    cotangent = scatter_about(arg_keys[1], (TOKENS, D), 1.0, 6.0, ((0, 16), (1, 2)))
    routes_keys = jax.random.split(jax.random.fold_in(arg_keys[2], 1), TOKENS // TOK_DEV)
    routes_turns = jax.random.permutation(jax.random.fold_in(arg_keys[2], 3), TOKENS // TOK_DEV)
    routes = jax.vmap(lambda own, number: assign_block(jax.random.fold_in(arg_keys[2], 2), own, number, TOK_DEV, EXPERTS, TOP, CAP, 2))(routes_keys, routes_turns).reshape((TOKENS, TOP))
    combine_weights = jnp.clip(0.2 + 0.8 * jax.random.uniform(arg_keys[3], (TOKENS, TOP), jnp.float32) ** shard_levels(arg_keys[3], (TOKENS, TOP), ((0, 16),), -0.2, 0.2), 0.2, 1.0)
    gate_weight = scatter_about(arg_keys[4], (EXPERTS, D, HID), D ** -0.5, 0.0625, ((0, 16), (1, 2)))
    up_weight = scatter_about(arg_keys[5], (EXPERTS, D, HID), D ** -0.5, 0.0625, ((0, 16), (1, 2)))
    down_weight = scatter_about(arg_keys[6], (EXPERTS, HID, D), HID ** -0.5, 0.1875, ((0, 16), (2, 2)))
    return {"tokens": tokens, "cotangent": cotangent, "routes": routes, "combine_weights": combine_weights, "gate_weight": gate_weight, "up_weight": up_weight, "down_weight": down_weight}


def block_sum(left_blocks, right_blocks, form):
    terms = jnp.einsum(form, left_blocks, right_blocks)
    rounded = lax.optimization_barrier(terms.astype(jnp.bfloat16))
    return jnp.sum(rounded.astype(jnp.float32), axis=1)


def expert_backward(x_rows, s_rows, weight_g, weight_u, weight_d):
    count = x_rows.shape[0]
    width = D // N_DP
    x_blocks = x_rows.reshape(count, N_DP, width).astype(jnp.float32)
    s_blocks = s_rows.reshape(count, N_DP, width).astype(jnp.float32)
    gate = block_sum(x_blocks, weight_g.reshape(N_DP, width, HID).astype(jnp.float32), "mbd,bdh->mbh")
    upper = block_sum(x_blocks, weight_u.reshape(N_DP, width, HID).astype(jnp.float32), "mbd,bdh->mbh")
    activation = jax.nn.silu(gate)
    hidden = (activation * upper).astype(jnp.bfloat16)
    dhidden = block_sum(s_blocks, weight_d.reshape(HID, N_DP, width).astype(jnp.float32), "mbd,hbd->mbh")
    sigmoid_g = jax.nn.sigmoid(gate)
    slope = sigmoid_g * (1.0 + gate * (1.0 - sigmoid_g))
    pre_gate = (dhidden * upper * slope).astype(jnp.bfloat16)
    pre_up = (dhidden * activation).astype(jnp.bfloat16)
    grad_down = jnp.dot(hidden.T, s_rows, preferred_element_type=jnp.float32).astype(jnp.bfloat16)
    grad_gate = jnp.dot(x_rows.T, pre_gate, preferred_element_type=jnp.float32).astype(jnp.bfloat16)
    grad_up = jnp.dot(x_rows.T, pre_up, preferred_element_type=jnp.float32).astype(jnp.bfloat16)
    back_rows = jnp.dot(pre_gate, weight_g.T, preferred_element_type=jnp.float32)
    back_rows = (back_rows + jnp.dot(pre_up, weight_u.T, preferred_element_type=jnp.float32)).astype(jnp.bfloat16)
    return grad_gate, grad_up, grad_down, back_rows


def fill_slots(slot_row, values):
    return jnp.zeros((EXPERTS * CAP, D), jnp.bfloat16).at[slot_row].set(values)


def pick_slots(buffer, slot_row):
    return buffer[slot_row]


def reference(tokens, cotangent, routes, combine_weights, gate_weight, up_weight, down_weight):
    pairs = TOK_DEV * TOP
    flat = routes.reshape(N_EXPERT, pairs).astype(jnp.int32)
    onehot = (flat[:, :, None] == jnp.arange(EXPERTS, dtype=jnp.int32)[None, None, :]).astype(jnp.int32)
    before = jnp.cumsum(onehot, axis=1) - onehot
    slot_rank = jnp.sum(before * onehot, axis=2)
    slots = (flat * CAP + slot_rank).astype(jnp.int32)
    scaled = (combine_weights[:, :, None] * cotangent[:, None, :].astype(jnp.float32)).astype(jnp.bfloat16)
    x_pairs = jnp.broadcast_to(tokens[:, None, :], (TOKENS, TOP, D)).reshape(N_EXPERT, pairs, D)
    s_pairs = scaled.reshape(N_EXPERT, pairs, D)
    send_x = jax.vmap(fill_slots)(slots, x_pairs)
    send_s = jax.vmap(fill_slots)(slots, s_pairs)
    by_x = send_x.reshape(N_EXPERT, EXPERTS, CAP, D).transpose(1, 0, 2, 3).reshape(EXPERTS, N_EXPERT * CAP, D)
    by_s = send_s.reshape(N_EXPERT, EXPERTS, CAP, D).transpose(1, 0, 2, 3).reshape(EXPERTS, N_EXPERT * CAP, D)

    def one_expert(packed):
        return expert_backward(packed[0], packed[1], packed[2], packed[3], packed[4])

    grad_gate, grad_up, grad_down, back_rows = lax.map(one_expert, (by_x, by_s, gate_weight, up_weight, down_weight))
    back = back_rows.reshape(EXPERTS, N_EXPERT, CAP, D).transpose(1, 0, 2, 3).reshape(N_EXPERT, EXPERTS * CAP, D)
    picked = jax.vmap(pick_slots)(back, slots)
    grad_tokens = jnp.sum(picked.reshape(TOKENS, TOP, D).astype(jnp.float32), axis=1).astype(jnp.bfloat16)
    return grad_tokens, grad_gate, grad_up, grad_down
```

```python
import jax
import jax.numpy as jnp
from jax import lax
from jax.sharding import PartitionSpec as P

F32 = jnp.float32
BF16 = jnp.bfloat16


def contract(left, right, left_dim, right_dim):
    return lax.dot_general(
        left, right, (((left_dim,), (right_dim,)), ((), ())), preferred_element_type=F32
    )


def batched(left, right, left_dim, right_dim):
    return lax.dot_general(
        left, right, (((left_dim,), (right_dim,)), ((0,), (0,))), preferred_element_type=F32
    )


def local(tokens, cotangent, routes, combine_weights, gate_weight, up_weight, down_weight):
    experts = lax.axis_size("expert")
    shards = lax.axis_size("dp")
    chips = experts // 2
    me = lax.axis_index("expert")
    core = me % 2
    tok_count = routes.shape[0]
    top_count = routes.shape[1]
    width = tokens.shape[1]
    capacity = 3 * tok_count * top_count // (2 * experts)
    rows = chips * capacity
    lanes = [list(range(0, experts, 2)), list(range(1, experts, 2))]
    swap = [(i, i ^ 1) for i in range(experts)]
    weight_g = gate_weight[0]
    weight_u = up_weight[0]
    weight_d = down_weight[0]

    def sibling(value):
        return lax.ppermute(value, "expert", swap)

    def gathered(value):
        own = lax.all_gather(value, "expert", axis_index_groups=lanes, axis=0, tiled=False)
        return own, sibling(own)

    def both_parts(part):
        if shards == 2:
            other = lax.ppermute(part, "dp", [(0, 1), (1, 0)])
            return part.astype(F32) + other.astype(F32)
        return jnp.sum(lax.all_gather(part, "dp").astype(F32), axis=0)

    all_routes = lax.all_gather(routes, "expert", axis=0).reshape(chips, 2, tok_count, top_count)
    all_weights = lax.all_gather(combine_weights, "expert", axis=0).reshape(
        chips, 2, tok_count, top_count
    )
    named = (all_routes == me).astype(F32)
    match = jnp.sum(named, axis=3)
    share = jnp.sum(named * all_weights, axis=3)
    rank = jnp.cumsum(match, axis=2) - match
    places = jnp.arange(capacity, dtype=jnp.int32).astype(F32)
    picks = (match[:, :, None, :] > 0) & (rank[:, :, None, :] == places[None, None, :, None])
    slot_share = jnp.sum(jnp.where(picks, share[:, :, None, :], 0.0), axis=3)
    picks = picks.astype(BF16)

    def side(value, which):
        return lax.dynamic_index_in_dim(value, which, axis=1, keepdims=False)

    pick = (side(picks, core), side(picks, 1 - core))
    factor = (side(slot_share, core), side(slot_share, 1 - core))

    x_blocks = gathered(tokens)
    rows_x = [
        batched(p, x, 2, 1).astype(BF16).reshape(rows, width) for p, x in zip(pick, x_blocks)
    ]
    rows_x = jnp.concatenate(rows_x, axis=0)
    cotangent, _ = lax.optimization_barrier((cotangent, x_blocks[0][0, :8, :128]))
    s_blocks = gathered(cotangent)
    gate_part = jnp.dot(rows_x, weight_g, preferred_element_type=F32).astype(BF16)
    up_part = jnp.dot(rows_x, weight_u, preferred_element_type=F32).astype(BF16)
    gate = both_parts(gate_part)
    upper = both_parts(up_part)
    rows_s = [
        (batched(p, s, 2, 1) * f[:, :, None]).astype(BF16).reshape(rows, width)
        for p, s, f in zip(pick, s_blocks, factor)
    ]
    rows_s = jnp.concatenate(rows_s, axis=0)
    dhidden = both_parts(contract(rows_s, weight_d, 1, 1).astype(BF16))

    activation = jax.nn.silu(gate)
    hidden = (activation * upper).astype(BF16)
    sigmoid_g = jax.nn.sigmoid(gate)
    slope = sigmoid_g * (1.0 + gate * (1.0 - sigmoid_g))
    pre_gate = (dhidden * upper * slope).astype(BF16)
    pre_up = (dhidden * activation).astype(BF16)

    pieces = []
    chunks = 2
    step = width // chunks
    for c in range(chunks):
        cols = slice(c * step, (c + 1) * step)
        back = (
            contract(pre_gate, weight_g[cols], 1, 1) + contract(pre_up, weight_u[cols], 1, 1)
        ).astype(BF16)
        back = back.reshape(2, chips, capacity, step)
        mine = batched(pick[0], back[0], 1, 1).astype(BF16)
        theirs = batched(pick[1], back[1], 1, 1).astype(BF16)
        chip_sum = (mine.astype(F32) + sibling(theirs).astype(F32)).astype(BF16)
        pieces.append(
            lax.psum_scatter(
                chip_sum, "expert", scatter_dimension=0, axis_index_groups=lanes, tiled=False
            )
        )
    grad_tokens = jnp.concatenate(pieces, axis=1)
    grad_down = contract(hidden, rows_s, 0, 0).astype(BF16)[None]
    grad_gate = contract(rows_x, pre_gate, 0, 0).astype(BF16)[None]
    grad_up = contract(rows_x, pre_up, 0, 0).astype(BF16)[None]
    return (grad_tokens, grad_gate, grad_up, grad_down)


def solution(mesh):
    placed = (
        P("expert", "dp"),
        P("expert", "dp"),
        P("expert", None),
        P("expert", None),
        P("expert", "dp", None),
        P("expert", "dp", None),
        P("expert", None, "dp"),
    )
    return jax.shard_map(
        local,
        mesh=mesh,
        in_specs=placed,
        out_specs=(
            P("expert", "dp"),
            P("expert", "dp", None),
            P("expert", "dp", None),
            P("expert", None, "dp"),
        ),
        check_vma=False,
    )
```

```python
import jax
import jax.numpy as jnp
import numpy as np
from jax import lax
from jax.sharding import PartitionSpec as P

F32 = jnp.float32
BF16 = jnp.bfloat16


def contract(left, right, left_dim, right_dim):
    return lax.dot_general(
        left, right, (((left_dim,), (right_dim,)), ((), ())), preferred_element_type=F32
    )


def after(value, *earlier):
    nothing = sum(jnp.minimum(jnp.abs(e[0, 0].astype(F32)), 0.0) for e in earlier)
    return (value.astype(F32) + nothing).astype(value.dtype)


def local(tokens, cotangent, routes, combine_weights, gate_weight, up_weight, down_weight):
    experts = lax.axis_size("expert")
    shards = lax.axis_size("dp")
    chips = experts // 2
    half = chips // 2
    me = lax.axis_index("expert")
    tok_count = routes.shape[0]
    top_count = routes.shape[1]
    width = tokens.shape[1]
    mid = width // 2
    capacity = 3 * tok_count * top_count // (2 * experts)
    lanes = [list(range(0, experts, 2)), list(range(1, experts, 2))]
    swap = [(i, i ^ 1) for i in range(experts)]
    ring = list(range(0, chips, 2)) + list(range(chips - 1, 0, -2))
    place = {chip: pos for pos, chip in enumerate(ring)}
    forward = [
        (2 * ring[p] + c, 2 * ring[(p + 1) % chips] + c) for p in range(chips) for c in range(2)
    ]
    backward = [(b, a) for a, b in forward]
    weight_g = gate_weight[0]
    weight_u = up_weight[0]
    weight_d = down_weight[0]

    def sibling(value):
        return lax.ppermute(value, "expert", swap)

    def ahead(value):
        return lax.ppermute(value, "expert", forward)

    def behind(value):
        return lax.ppermute(value, "expert", backward)

    def both_parts(part):
        total, term = part.astype(F32), part
        for _ in range(shards - 1):
            term = lax.ppermute(term, "dp", [(i, (i + 1) % shards) for i in range(shards)])
            total = total + term.astype(F32)
        return total

    near = [0] + [s * d for d in range(1, half - 1) for s in (1, -1)]
    far = [half - 1, 1 - half, half]
    groups = [near, far]
    offsets = near + far

    packed = jnp.concatenate([routes.T.astype(F32), combine_weights.T], axis=0)
    packed = lax.all_gather(packed, "expert", axis_index_groups=lanes, axis=0, tiled=False)
    table = np.array(
        [[ring[(place[chip] - d) % chips] for d in offsets] for chip in range(chips)], np.int32
    )
    packed = jnp.take(packed, jnp.asarray(table)[me // 2], axis=0)
    lane_routes, lane_weights = packed[:, :top_count], packed[:, top_count:]
    wanted = jnp.stack([me, me ^ 1]).astype(F32)
    named = (lane_routes[:, None] == wanted[None, :, None, None]).astype(F32)
    match = jnp.sum(named, axis=2)
    share = jnp.sum(named * lane_weights[:, None], axis=2)
    rank = jnp.cumsum(match, axis=2) - match
    places = jnp.arange(capacity, dtype=jnp.int32).astype(F32)
    picks = (match[:, :, None, :] > 0) & (rank[:, :, None, :] == places[None, None, :, None])
    factors = jnp.sum(jnp.where(picks, share[:, :, None, :], 0.0), axis=3)
    picks = picks.astype(BF16)

    def gathered(block):
        blocks = {0: block}
        fore, back = block, block
        for d in range(1, half):
            fore, back = ahead(fore), behind(back)
            blocks[d], blocks[-d] = fore, back
        blocks[half] = (ahead(fore[:, :mid]), behind(back[:, mid:]))
        return blocks

    def picked(blocks, group, scaled):
        mine, other = [], []
        for d in group:
            i = offsets.index(d)
            pick = picks[i].reshape(2 * capacity, tok_count)
            factor = factors[i].reshape(2 * capacity, 1)

            def choose(block):
                rows = contract(pick, block, 1, 0)
                return (rows * factor if scaled else rows).astype(BF16)

            if isinstance(blocks[d], tuple):
                rows = jnp.concatenate([choose(b) for b in blocks[d]], axis=1)
            else:
                rows = choose(blocks[d])
            mine.append(rows[:capacity])
            other.append(rows[capacity:])
        return jnp.concatenate(mine + [sibling(jnp.concatenate(other, axis=0))], axis=0)

    x_blocks = gathered(tokens)
    s_blocks = gathered(after(cotangent, x_blocks[half - 1], x_blocks[1 - half]))

    rows_x = [picked(x_blocks, group, False) for group in groups]
    gate = [both_parts(contract(x, weight_g, 1, 0).astype(BF16)) for x in rows_x]
    upper = [both_parts(contract(x, weight_u, 1, 0).astype(BF16)) for x in rows_x]
    rows_s = [picked(s_blocks, group, True) for group in groups]
    dhidden = [both_parts(contract(s, weight_d, 1, 1).astype(BF16)) for s in rows_s]

    hidden, pre_gate, pre_up, back = [], [], [], []
    for g, u, dh in zip(gate, upper, dhidden):
        activation = jax.nn.silu(g)
        sigmoid_g = jax.nn.sigmoid(g)
        slope = sigmoid_g * (1.0 + g * (1.0 - sigmoid_g))
        hidden.append((activation * u).astype(BF16))
        pre_gate.append((dh * u * slope).astype(BF16))
        pre_up.append((dh * activation).astype(BF16))

    returned = {}
    for which in (1, 0):
        rows = (
            contract(pre_gate[which], weight_g, 1, 1) + contract(pre_up[which], weight_u, 1, 1)
        ).astype(BF16)
        count = len(groups[which]) * capacity
        mine, other = rows[:count], sibling(rows[count:])
        for k, d in enumerate(groups[which]):
            span = slice(k * capacity, (k + 1) * capacity)
            returned[d] = (mine[span], other[span])

    def term(d, lo, hi):
        i = offsets.index(d)
        pair = jnp.concatenate([r[:, lo:hi] for r in returned[d]], axis=0)
        return contract(picks[i].reshape(2 * capacity, tok_count), pair, 0, 0)

    arrivals = []

    def reduced(lo, hi):
        cut = (lo + hi) // 2
        fore = behind(term(half, lo, cut).astype(BF16))
        back = ahead(term(half, cut, hi).astype(BF16))
        landed = (fore, back)
        fore = jnp.pad(fore, ((0, 0), (0, hi - cut)))
        back = jnp.pad(back, ((0, 0), (cut - lo, 0)))
        for d in range(half - 1, 0, -1):
            arrivals.append(landed)
            fore = behind((term(d, lo, hi) + fore.astype(F32)).astype(BF16))
            back = ahead((term(-d, lo, hi) + back.astype(F32)).astype(BF16))
            landed = (fore, back)
        return (term(0, lo, hi) + fore.astype(F32) + back.astype(F32)).astype(BF16)

    grad_tokens = jnp.concatenate([reduced(0, mid), reduced(mid, width)], axis=1)

    hidden, pre_gate, pre_up, rows_x, rows_s = (
        jnp.concatenate(v, axis=0) for v in (hidden, pre_gate, pre_up, rows_x, rows_s)
    )
    first, second, third = (arrivals[min(k, half - 2)] for k in range(3))
    grad_gate = contract(rows_x, after(pre_gate, *first), 0, 0).astype(BF16)[None]
    grad_up = contract(rows_x, after(pre_up, *second), 0, 0).astype(BF16)[None]
    grad_down = contract(after(hidden, *third), rows_s, 0, 0).astype(BF16)[None]
    return (grad_tokens, grad_gate, grad_up, grad_down)


def solution(mesh):
    placed = (
        P("expert", "dp"),
        P("expert", "dp"),
        P("expert", None),
        P("expert", None),
        P("expert", "dp", None),
        P("expert", "dp", None),
        P("expert", None, "dp"),
    )
    return jax.shard_map(
        local,
        mesh=mesh,
        in_specs=placed,
        out_specs=(
            P("expert", "dp"),
            P("expert", "dp", None),
            P("expert", "dp", None),
            P("expert", None, "dp"),
        ),
        check_vma=False,
    )
```
